256 devices in a mesh: section: 8 (over z_lo, y), seq: 32 (over x, z_hi, core).
Axes of the slice: x: 4, y: 4, z: 8 (z_hi: 4, z_lo: 2; z = z_hi * 2 + z_lo), core: 2. Of those that a mesh axis runs over, the one named last changes fastest.
Arguments:
- qkv: bfloat16 [8, 4096, 3, 4096], P('section', 'seq'), may hold values from -20 to 20
- scale_exp: int32 [8, 32, 3, 32], P('section', 'seq'), may hold values from -1 to 2
- residual_in: bfloat16 [8, 4096, 4096], P('section', 'seq'), may hold values from -6 to 6
- skip_in: bfloat16 [8, 4096, 4096], P('section', 'seq'), may hold values from -6 to 6
- skip_gain: float32 [4096], replicated, may hold values from 0.1 to 1.9
Outputs:
- combined: bfloat16 [8, 4096, 4096], P('section', 'seq')
The draws below stay inside these ranges and needn't reach their ends.
All inputs are finite; a program needn't handle non-finite values.
Results may differ from the reference program's by a relative error of at most 0.0045.
Values may be sent and summed in bfloat16 or wider, within the bound.
A program may use at most 64 MiB of HBM per device.

```python
import math
import jax
import jax.numpy as jnp
from jax import lax

HS = 128
HEADS = 32
BLOCK = 128
HD = 4096
TOKENS = 4096
N_SECTION = 8


def draw_qkv(key, part):
    key = jax.random.fold_in(key, 11)
    base = jax.random.truncated_normal(key, -6.0, 6.0, (N_SECTION, TOKENS, 3, HEADS * HS), jnp.float32)
    return jnp.clip(base, -20.0, 20.0).astype(jnp.bfloat16)


def plant(entries, key, low, high):
    longest = entries.shape.index(max(entries.shape))
    spots = []
    for shift in (0, 1):
        where = [jax.random.randint(jax.random.fold_in(key, axis), (), 0, length) for axis, length in enumerate(entries.shape)]
        where[longest] = (where[longest] + shift) % entries.shape[longest]
        spots.append(tuple(where))
    return entries.at[spots[0]].set(low).at[spots[1]].set(high)


def block_levels(stream_key, dims, pieces, least, largest):
    def one(dim, shards_of):
        heights = jax.random.uniform(jax.random.fold_in(jax.random.fold_in(stream_key, 6), dim), (shards_of,), jnp.float32, least / len(pieces), largest / len(pieces))
        return jnp.repeat(jnp.exp(heights), dims[dim] // shards_of).reshape((-1,) + (1,) * (len(dims) - dim - 1))

    level = one(*pieces[0])
    for cut in pieces[1:]:
        level = level * one(*cut)
    return level


def scatter_about(rng, extent, deviation, bound, shards=(), held_as=jnp.bfloat16):
    array = deviation * jax.random.normal(rng, extent, jnp.float32)
    if shards:
        array = array * block_levels(rng, extent, shards, -0.22, 0.18)
    return jnp.clip(array, -bound, bound).astype(held_as)


def setup_inputs(seed: int = 0) -> dict:
    keys = jax.random.split(jax.random.key(seed), 6)
    return {
        "qkv": draw_qkv(jax.random.fold_in(keys[5], 71), 0),
        "scale_exp": plant(jax.random.randint(keys[1], (N_SECTION, TOKENS // BLOCK, 3, HEADS), -1, 3), jax.random.fold_in(keys[1], 1), -1, 2).astype(jnp.int32),
        "residual_in": scatter_about(keys[2], (N_SECTION, TOKENS, HD), 1.0, 6.0, ((0, 8), (1, 32))),
        "skip_in": scatter_about(keys[3], (N_SECTION, TOKENS, HD), 1.0, 6.0, ((0, 8), (1, 32))),
        "skip_gain": jnp.clip(1.0 + 0.18 * jax.random.normal(keys[4], (HD,), jnp.float32), 0.1, 1.9),
    }


def reference(qkv, scale_exp, residual_in, skip_in, skip_gain):
    factor = jnp.exp2(scale_exp.astype(jnp.float32))
    factor = jnp.repeat(factor, BLOCK, axis=1)
    factor = jnp.repeat(factor, HS, axis=3)
    scaled = (qkv.astype(jnp.float32) * factor).astype(jnp.bfloat16)
    score_scale = 1.0 / math.sqrt(HS)

    def one_head(triple):
        query_rows, key_rows, value_rows = triple
        scores = jnp.dot(query_rows, key_rows.T, preferred_element_type=jnp.float32) * score_scale
        weights = jax.nn.softmax(scores, axis=-1).astype(jnp.bfloat16)
        return jnp.dot(weights, value_rows, preferred_element_type=jnp.float32).astype(jnp.bfloat16)

    def one_section(group):
        split_heads = group.reshape(TOKENS, 3, HEADS, HS).transpose(1, 2, 0, 3)
        result = lax.map(one_head, (split_heads[0], split_heads[1], split_heads[2]))
        return result.transpose(1, 0, 2).reshape(TOKENS, HEADS * HS)
    attended = lax.map(one_section, scaled)
    incoming = jnp.roll(residual_in, 1, axis=0)
    mirrored = skip_in[::-1]
    combined = incoming.astype(jnp.float32) + skip_gain * mirrored.astype(jnp.float32) + attended.astype(jnp.float32)
    return combined.astype(jnp.bfloat16)
```

```python
import math

import jax
import jax.numpy as jnp
from jax import lax
from jax.experimental import pallas as pl
from jax.experimental.pallas import tpu as pltpu
from jax.sharding import PartitionSpec as P

MESH = pl.DeviceIdType.MESH
PEERS = 32
HS = 128
ROWS = 128
TOKENS = PEERS * ROWS
HD = PEERS * HS
SECTIONS = 8
GROUP = 2
QB = GROUP * ROWS
KB = 512
LOG2E = math.log2(math.e)
SCORE = LOG2E / math.sqrt(HS)


def pick(i, values):
    out = values[-1]
    for n in range(len(values) - 2, -1, -1):
        out = jnp.where(i == n, values[n], out)
    return out


def offsets(slot):
    return pick((slot // 4) % 4, (2, 1, 3, 0)), pick(slot % 4, (1, 3, 2, 0)), 1 - slot // 16


def target(seq, slot):
    dx, dz, dc = offsets(slot)
    return ((seq // 8 + dx) % 4) * 8 + ((seq // 2 + dz) % 4) * 2 + (seq + dc) % 2


def origin(seq, slot):
    dx, dz, dc = offsets(slot)
    return ((seq // 8 + 4 - dx) % 4) * 8 + ((seq // 2 + 4 - dz) % 4) * 2 + (seq + dc) % 2


def kernel(
    exps, qkv_hbm, res_hbm, skip_hbm, gain, out,
    qkv, kv_out, q_out, kv_in, q_in, o_out, o_in, res_in, skip_in, own_a, own_b, scores,
    load_sem, own_sem, kv_send, kv_recv, q_send, q_recv, o_send, o_recv, res_sem, skip_sem,
):
    sec = lax.axis_index("section")
    seq = lax.axis_index("seq")
    nxt = (sec + 1) % SECTIONS
    prv = (sec + SECTIONS - 1) % SECTIONS
    mir = SECTIONS - 1 - sec
    sums = nxt == mir
    summed = prv == mir

    load = pltpu.make_async_copy(qkv_hbm, qkv, load_sem)
    load.start()
    barrier = pltpu.get_barrier_semaphore()

    def greet(k, _):
        pl.semaphore_signal(barrier, inc=1, device_id=(sec, target(seq, k)), device_id_type=MESH)
        return 0

    lax.fori_loop(0, PEERS - 1, greet, 0)
    for s in (nxt, prv, mir):
        pl.semaphore_signal(barrier, inc=1, device_id=(s, seq), device_id_type=MESH)

    own_res = pltpu.make_async_copy(res_hbm, own_a, own_sem.at[0])
    own_skip = pltpu.make_async_copy(skip_hbm, own_b, own_sem.at[1])
    own_res.start()
    own_skip.start()
    load.wait()

    def scale(k, _):
        head = target(seq, k)
        cols = pl.ds(pl.multiple_of(head * HS, HS), HS)
        for c in range(3):
            power = jnp.left_shift(jnp.int32(1), exps[c, head] + 8).astype(jnp.float32) * (2.0**-8)
            part = (qkv[c, :, cols].astype(jnp.float32) * power).astype(jnp.bfloat16)
            if c == 0:
                q_out[k] = part
            else:
                kv_out[k, c - 1] = part
        return 0

    lax.fori_loop(0, PEERS, scale, 0)
    kv_in[PEERS - 1] = kv_out[PEERS - 1]
    q_in[PEERS - 1] = q_out[PEERS - 1]
    own_res.wait()
    own_skip.wait()

    @pl.when(sums)
    def _():
        def add(i, _):
            rows = pl.ds(pl.multiple_of(i * 16, 16), 16)
            both = own_a[rows, :].astype(jnp.float32) + gain[...] * own_b[rows, :].astype(jnp.float32)
            own_a[rows, :] = both.astype(jnp.bfloat16)
            return 0

        lax.fori_loop(0, ROWS // 16, add, 0)

    pl.semaphore_wait(barrier, PEERS - 1 + 3)

    def kv_copy(k):
        return pltpu.make_async_remote_copy(
            src_ref=kv_out.at[k], dst_ref=kv_in.at[k], send_sem=kv_send.at[k], recv_sem=kv_recv.at[k],
            device_id=(sec, target(seq, k)), device_id_type=MESH,
        )

    def q_copy(k):
        return pltpu.make_async_remote_copy(
            src_ref=q_out.at[k], dst_ref=q_in.at[k], send_sem=q_send.at[k], recv_sem=q_recv.at[k],
            device_id=(sec, target(seq, k)), device_id_type=MESH,
        )

    def o_copy(k):
        return pltpu.make_async_remote_copy(
            src_ref=o_out.at[k], dst_ref=o_in.at[k], send_sem=o_send.at[k], recv_sem=o_recv.at[k],
            device_id=(sec, origin(seq, k)), device_id_type=MESH,
        )

    res_copy = pltpu.make_async_remote_copy(
        src_ref=own_a, dst_ref=res_in, send_sem=res_sem.at[0], recv_sem=res_sem.at[1],
        device_id=(nxt, seq), device_id_type=MESH,
    )

    def skip_copy(i):
        rows = pl.ds(pl.multiple_of(i * 16, 16), 16)
        return pltpu.make_async_remote_copy(
            src_ref=own_b.at[rows], dst_ref=skip_in.at[rows], send_sem=skip_sem.at[0, i], recv_sem=skip_sem.at[1, i],
            device_id=(mir, seq), device_id_type=MESH,
        )

    def start_kv(k, _):
        kv_copy(k).start()
        return 0

    def start_q(k, _):
        q_copy(k).start()
        return 0

    lax.fori_loop(0, PEERS - 1, start_kv, 0)
    res_copy.start()
    lax.fori_loop(0, PEERS - 1, start_q, 0)

    def take_kv(k, _):
        kv_copy(k).wait_recv()
        return 0

    lax.fori_loop(0, PEERS - 1, take_kv, 0)

    def attend(g, _):
        first = g * GROUP
        for n in range(GROUP):

            @pl.when(first + n < PEERS - 1)
            def _():
                q_copy(first + n).wait_recv()

        q = q_in[pl.ds(first, GROUP)].reshape(QB, HS)
        most = None
        for j in range(TOKENS // KB):
            keys = kv_in[j * KB // ROWS : (j + 1) * KB // ROWS, 0].reshape(KB, HS)
            s = lax.dot_general(q, keys, (((1,), (1,)), ((), ())), preferred_element_type=jnp.float32)
            scores[:, j * KB : (j + 1) * KB] = s
            for u in range(KB // 128):
                t = s[:, u * 128 : (u + 1) * 128]
                most = t if most is None else jnp.maximum(most, t)
        top = jnp.max(most, axis=1, keepdims=True) * SCORE
        acc = jnp.zeros((QB, HS), jnp.float32)
        total = jnp.zeros((QB, 128), jnp.float32)
        for j in range(TOKENS // KB):
            values = kv_in[j * KB // ROWS : (j + 1) * KB // ROWS, 1].reshape(KB, HS)
            p = jnp.exp2(scores[:, j * KB : (j + 1) * KB] * SCORE - top)
            for u in range(KB // 128):
                total = total + p[:, u * 128 : (u + 1) * 128]
            acc = acc + jnp.dot(p.astype(jnp.bfloat16), values, preferred_element_type=jnp.float32)
        done = (acc / jnp.sum(total, axis=1, keepdims=True)).astype(jnp.bfloat16)
        o_out[pl.ds(first, GROUP)] = done.reshape(GROUP, ROWS, HS)
        for n in range(GROUP):

            @pl.when(first + n < PEERS - 1)
            def _():
                o_copy(first + n).start()

        @pl.when(jnp.logical_and(g < 8, jnp.logical_not(sums)))
        def _():
            skip_copy(g).start()

        return 0

    lax.fori_loop(0, PEERS // GROUP, attend, 0)
    o_in[PEERS - 1] = o_out[PEERS - 1]

    res_copy.wait_recv()

    @pl.when(jnp.logical_not(summed))
    def _():
        def take_skip(i, _):
            skip_copy(i).wait_recv()
            return 0

        lax.fori_loop(0, 8, take_skip, 0)

    def finish(k, _):
        @pl.when(k < PEERS - 1)
        def _():
            o_copy(k).wait_recv()

        cols = pl.ds(pl.multiple_of(target(seq, k) * HS, HS), HS)
        base = res_in[:, cols].astype(jnp.float32)

        @pl.when(summed)
        def _():
            out[:, cols] = (base + o_in[k].astype(jnp.float32)).astype(jnp.bfloat16)

        @pl.when(jnp.logical_not(summed))
        def _():
            both = base + gain[:, cols] * skip_in[:, cols].astype(jnp.float32)
            out[:, cols] = (both + o_in[k].astype(jnp.float32)).astype(jnp.bfloat16)

        return 0

    lax.fori_loop(0, PEERS, finish, 0)

    def sent(k, _):
        kv_copy(k).wait_send()
        q_copy(k).wait_send()
        o_copy(k).wait_send()
        return 0

    lax.fori_loop(0, PEERS - 1, sent, 0)
    res_copy.wait_send()

    @pl.when(jnp.logical_not(sums))
    def _():
        def sent_skip(i, _):
            skip_copy(i).wait_send()
            return 0

        lax.fori_loop(0, 8, sent_skip, 0)


def body(qkv, scale_exp, residual_in, skip_in, skip_gain):
    bf16 = jnp.bfloat16
    block = pltpu.VMEM((PEERS, ROWS, HS), bf16)
    pair = pltpu.VMEM((PEERS, 2, ROWS, HS), bf16)
    rows = pltpu.VMEM((ROWS, HD), bf16)
    sems = pltpu.SemaphoreType.DMA((PEERS,))
    anywhere = pl.BlockSpec(memory_space=pl.ANY)
    vmem = pl.BlockSpec(memory_space=pltpu.VMEM)
    combined = pl.pallas_call(
        kernel,
        out_shape=jax.ShapeDtypeStruct((ROWS, HD), bf16),
        in_specs=[pl.BlockSpec(memory_space=pltpu.SMEM), anywhere, anywhere, anywhere, vmem],
        out_specs=vmem,
        scratch_shapes=[
            pltpu.VMEM((3, ROWS, HD), bf16), pair, block, pair, block, block, block, rows, rows, rows, rows,
            pltpu.VMEM((QB, TOKENS), jnp.float32),
            pltpu.SemaphoreType.DMA, pltpu.SemaphoreType.DMA((2,)), sems, sems, sems, sems, sems, sems,
            pltpu.SemaphoreType.DMA((2,)), pltpu.SemaphoreType.DMA((2, 8)),
        ],
        compiler_params=pltpu.CompilerParams(
            collective_id=0, has_side_effects=True, vmem_limit_bytes=56 * 2**20
        ),
    )(
        scale_exp.reshape(3, PEERS),
        qkv[0].transpose(1, 0, 2),
        residual_in[0],
        skip_in[0],
        skip_gain.reshape(1, HD),
    )
    return combined[None]


def solution(mesh):
    return jax.shard_map(
        body,
        mesh=mesh,
        in_specs=(
            P("section", "seq", None, None),
            P("section", "seq", None, None),
            P("section", "seq", None),
            P("section", "seq", None),
            P(),
        ),
        out_specs=P("section", "seq", None),
        check_vma=False,
    )
```

```python
import math

import jax
import jax.numpy as jnp
from jax import lax
from jax.experimental import pallas as pl
from jax.experimental.pallas import tpu as pltpu
from jax.sharding import PartitionSpec as P

MESH = pl.DeviceIdType.MESH
PEERS = 32
HS = 128
ROWS = 128
TOKENS = PEERS * ROWS
HD = PEERS * HS
SECTIONS = 8
RELAYED = 16
LAG = 10
CHUNK_GROUP = 4
CHUNKS = 8
GROUP = 2
QB = GROUP * ROWS
KB = 512
LOG2E = math.log2(math.e)
SCORE = LOG2E / math.sqrt(HS)


def pick(i, values):
    out = values[-1]
    for n in range(len(values) - 2, -1, -1):
        out = jnp.where(i == n, values[n], out)
    return out


def offsets(slot):
    dz = jnp.where(slot < RELAYED, 2 - slot % 2, 3 - 3 * (slot % 2))
    return pick((slot // 2) % 4, (2, 1, 3, 0)), dz, 1 - (slot // 8) % 2


def shifted(seq, slot, sign, way):
    dx, dz, dc = offsets(slot)
    x, z, core = seq // 8, (seq // 2) % 4, seq % 2
    return ((x + 4 + way * dx) % 4) * 8 + ((z + 4 + way * sign * dz) % 4) * 2 + (core + dc) % 2


def target(seq, slot, sign):
    return shifted(seq, slot, sign, 1)


def origin(seq, slot, sign):
    return shifted(seq, slot, sign, -1)


def kernel(
    exps, qkv_hbm, res_hbm, skip_hbm, gain, out,
    qkv, kv_out, q_out, kv_in, q_in, o_out, o_in, passed, res_in, skip_in, own_a, own_b, both, scores,
    load_sem, own_sem, kv_send, kv_recv, q_send, q_recv, o_send, o_recv, pass_send, res_sem, skip_sem,
):
    sec = lax.axis_index("section")
    seq = lax.axis_index("seq")
    nxt = (sec + 1) % SECTIONS
    prv = (sec + SECTIONS - 1) % SECTIONS
    mir = SECTIONS - 1 - sec
    sign = 1 - 2 * (sec // 4)
    sums = nxt == mir
    summed = prv == mir

    load = pltpu.make_async_copy(qkv_hbm, qkv, load_sem)
    load.start()
    barrier = pltpu.get_barrier_semaphore()

    def greet(k, _):
        pl.semaphore_signal(barrier, inc=1, device_id=(sec, target(seq, k, sign)), device_id_type=MESH)
        return 0

    def greet_relay(k, _):
        pl.semaphore_signal(barrier, inc=1, device_id=(mir, origin(seq, k, sign)), device_id_type=MESH)
        return 0

    lax.fori_loop(0, PEERS - 1, greet, 0)
    lax.fori_loop(0, RELAYED, greet_relay, 0)
    for s in (nxt, prv, mir):
        pl.semaphore_signal(barrier, inc=1, device_id=(s, seq), device_id_type=MESH)

    own_res = pltpu.make_async_copy(res_hbm, own_a, own_sem.at[0])
    own_skip = pltpu.make_async_copy(skip_hbm, own_b, own_sem.at[1])
    own_res.start()
    own_skip.start()
    load.wait()

    def scale(k, _):
        head = target(seq, k, sign)
        cols = pl.ds(pl.multiple_of(head * HS, HS), HS)
        for c in range(3):
            power = jnp.left_shift(jnp.int32(1), exps[c, head] + 8).astype(jnp.float32) * (2.0**-8)
            part = (qkv[c, :, cols].astype(jnp.float32) * power).astype(jnp.bfloat16)
            if c == 0:
                q_out[k] = part
            else:
                kv_out[k, c - 1] = part
        return 0

    lax.fori_loop(0, PEERS, scale, 0)
    kv_in[PEERS - 1] = kv_out[PEERS - 1]
    q_in[PEERS - 1] = q_out[PEERS - 1]
    own_res.wait()
    own_skip.wait()

    @pl.when(sums)
    def _():
        def add(i, _):
            rows = pl.ds(pl.multiple_of(i * 16, 16), 16)
            total = own_a[rows, :].astype(jnp.float32) + gain[...] * own_b[rows, :].astype(jnp.float32)
            both[rows, :] = total.astype(jnp.bfloat16)
            return 0

        lax.fori_loop(0, ROWS // 16, add, 0)

    pl.semaphore_wait(barrier, PEERS - 1 + RELAYED + 3)

    def kv_copy(k):
        return pltpu.make_async_remote_copy(
            src_ref=kv_out.at[k], dst_ref=kv_in.at[k], send_sem=kv_send.at[k], recv_sem=kv_recv.at[k],
            device_id=(sec, target(seq, k, sign)), device_id_type=MESH,
        )

    def q_copy(k):
        return pltpu.make_async_remote_copy(
            src_ref=q_out.at[k], dst_ref=q_in.at[k], send_sem=q_send.at[k], recv_sem=q_recv.at[k],
            device_id=(sec, target(seq, k, sign)), device_id_type=MESH,
        )

    def o_copy(k):
        relayed = k < RELAYED
        land = jnp.where(relayed, PEERS + k, k)
        return pltpu.make_async_remote_copy(
            src_ref=o_out.at[k], dst_ref=o_in.at[land], send_sem=o_send.at[k], recv_sem=o_recv.at[land],
            device_id=(jnp.where(relayed, mir, sec), origin(seq, k, sign)), device_id_type=MESH,
        )

    def pass_copy(k):
        return pltpu.make_async_remote_copy(
            src_ref=passed.at[k], dst_ref=o_in.at[k], send_sem=pass_send.at[k], recv_sem=o_recv.at[k],
            device_id=(mir, seq), device_id_type=MESH,
        )

    def arrived(slot):
        pltpu.make_async_copy(o_in.at[slot], o_in.at[slot], o_recv.at[slot]).wait()

    res_copy = pltpu.make_async_remote_copy(
        src_ref=own_a, dst_ref=res_in, send_sem=res_sem.at[0], recv_sem=res_sem.at[1],
        device_id=(nxt, seq), device_id_type=MESH,
    )

    def chunk_copy(i, src, dst):
        z = (seq // 2 + 4 - 3 * sign * (i % 2)) % 4
        cols = pl.ds(pl.multiple_of(((i // 2) * 8 + z * 2) * HS, 2 * HS), 2 * HS)
        return pltpu.make_async_remote_copy(
            src_ref=src.at[:, cols], dst_ref=dst.at[:, cols], send_sem=skip_sem.at[0, i], recv_sem=skip_sem.at[1, i],
            device_id=(mir, seq), device_id_type=MESH,
        )

    def relay(k):
        arrived(PEERS + k)
        cols = pl.ds(pl.multiple_of(target(seq, k, -sign) * HS, HS), HS)
        part = o_in[PEERS + k].astype(jnp.float32) + gain[:, cols] * own_b[:, cols].astype(jnp.float32)

        @pl.when(sums)
        def _():
            passed[k] = (part + own_a[:, cols].astype(jnp.float32)).astype(jnp.bfloat16)

        @pl.when(jnp.logical_not(sums))
        def _():
            passed[k] = part.astype(jnp.bfloat16)

        pass_copy(k).start()

    def start_kv(k, _):
        kv_copy((k % 2) * RELAYED + k // 2).start()
        return 0

    def start_q(k, _):
        q_copy(k).start()
        return 0

    lax.fori_loop(0, PEERS - 1, start_kv, 0)

    @pl.when(jnp.logical_not(sums))
    def _():
        res_copy.start()

    lax.fori_loop(0, PEERS - 1, start_q, 0)

    def take_kv(k, _):
        kv_copy(k).wait_recv()
        return 0

    lax.fori_loop(0, PEERS - 1, take_kv, 0)

    def attend(g, _):
        first = g * GROUP
        for n in range(GROUP):

            @pl.when(first + n < PEERS - 1)
            def _():
                q_copy(first + n).wait_recv()

        q = q_in[pl.ds(first, GROUP)].reshape(QB, HS)
        most = None
        for j in range(TOKENS // KB):
            keys = kv_in[j * KB // ROWS : (j + 1) * KB // ROWS, 0].reshape(KB, HS)
            s = lax.dot_general(q, keys, (((1,), (1,)), ((), ())), preferred_element_type=jnp.float32)
            scores[:, j * KB : (j + 1) * KB] = s
            for u in range(KB // 128):
                t = s[:, u * 128 : (u + 1) * 128]
                most = t if most is None else jnp.maximum(most, t)
        top = jnp.max(most, axis=1, keepdims=True) * SCORE
        acc = jnp.zeros((QB, HS), jnp.float32)
        total = jnp.zeros((QB, 128), jnp.float32)
        for j in range(TOKENS // KB):
            values = kv_in[j * KB // ROWS : (j + 1) * KB // ROWS, 1].reshape(KB, HS)
            p = jnp.exp2(scores[:, j * KB : (j + 1) * KB] * SCORE - top)
            for u in range(KB // 128):
                total = total + p[:, u * 128 : (u + 1) * 128]
            acc = acc + jnp.dot(p.astype(jnp.bfloat16), values, preferred_element_type=jnp.float32)
        done = (acc / jnp.sum(total, axis=1, keepdims=True)).astype(jnp.bfloat16)
        o_out[pl.ds(first, GROUP)] = done.reshape(GROUP, ROWS, HS)
        for n in range(GROUP):

            @pl.when(first + n < PEERS - 1)
            def _():
                o_copy(first + n).start()

        @pl.when(jnp.logical_and(jnp.logical_and(g >= CHUNK_GROUP, g < CHUNK_GROUP + CHUNKS), sums))
        def _():
            chunk_copy(g - CHUNK_GROUP, both, res_in).start()

        @pl.when(jnp.logical_and(jnp.logical_and(g >= CHUNK_GROUP, g < CHUNK_GROUP + CHUNKS), jnp.logical_not(sums)))
        def _():
            chunk_copy(g - CHUNK_GROUP, own_b, skip_in).start()

        @pl.when(g >= LAG)
        def _():
            for n in range(GROUP):
                relay((g - LAG) * GROUP + n)

        return 0

    lax.fori_loop(0, PEERS // GROUP, attend, 0)

    def relay_late(k, _):
        relay(k)
        return 0

    lax.fori_loop(PEERS - LAG * GROUP, RELAYED, relay_late, 0)
    o_in[PEERS - 1] = o_out[PEERS - 1]

    @pl.when(jnp.logical_not(summed))
    def _():
        res_copy.wait_recv()

    def take_chunk(i, _):
        chunk_copy(i, own_b, skip_in).wait_recv()
        return 0

    lax.fori_loop(0, CHUNKS, take_chunk, 0)

    def finish(k, _):
        @pl.when(k < PEERS - 1)
        def _():
            arrived(k)

        cols = pl.ds(pl.multiple_of(target(seq, k, sign) * HS, HS), HS)
        done = o_in[k].astype(jnp.float32)

        @pl.when(jnp.logical_and(summed, k < RELAYED))
        def _():
            out[:, cols] = o_in[k]

        @pl.when(jnp.logical_xor(summed, k < RELAYED))
        def _():
            out[:, cols] = (res_in[:, cols].astype(jnp.float32) + done).astype(jnp.bfloat16)

        @pl.when(jnp.logical_and(jnp.logical_not(summed), k >= RELAYED))
        def _():
            rest = res_in[:, cols].astype(jnp.float32) + gain[:, cols] * skip_in[:, cols].astype(jnp.float32)
            out[:, cols] = (rest + done).astype(jnp.bfloat16)

        return 0

    lax.fori_loop(RELAYED, PEERS, finish, 0)
    lax.fori_loop(0, RELAYED, finish, 0)

    def sent(k, _):
        kv_copy(k).wait_send()
        q_copy(k).wait_send()
        o_copy(k).wait_send()
        return 0

    def sent_more(k, _):
        pass_copy(k).wait_send()
        return 0

    def sent_chunk(i, _):
        chunk_copy(i, own_b, skip_in).wait_send()
        return 0

    lax.fori_loop(0, PEERS - 1, sent, 0)
    lax.fori_loop(0, RELAYED, sent_more, 0)
    lax.fori_loop(0, CHUNKS, sent_chunk, 0)

    @pl.when(jnp.logical_not(sums))
    def _():
        res_copy.wait_send()


def body(qkv, scale_exp, residual_in, skip_in, skip_gain):
    bf16 = jnp.bfloat16
    block = pltpu.VMEM((PEERS, ROWS, HS), bf16)
    pair = pltpu.VMEM((PEERS, 2, ROWS, HS), bf16)
    rows = pltpu.VMEM((ROWS, HD), bf16)
    sems = pltpu.SemaphoreType.DMA((PEERS,))
    anywhere = pl.BlockSpec(memory_space=pl.ANY)
    vmem = pl.BlockSpec(memory_space=pltpu.VMEM)
    combined = pl.pallas_call(
        kernel,
        out_shape=jax.ShapeDtypeStruct((ROWS, HD), bf16),
        in_specs=[pl.BlockSpec(memory_space=pltpu.SMEM), anywhere, anywhere, anywhere, vmem],
        out_specs=vmem,
        scratch_shapes=[
            pltpu.VMEM((3, ROWS, HD), bf16), pair, block, pair, block, block,
            pltpu.VMEM((PEERS + RELAYED, ROWS, HS), bf16), pltpu.VMEM((RELAYED, ROWS, HS), bf16), rows, rows, rows, rows, rows,
            pltpu.VMEM((QB, TOKENS), jnp.float32),
            pltpu.SemaphoreType.DMA, pltpu.SemaphoreType.DMA((2,)), sems, sems, sems, sems, sems,
            pltpu.SemaphoreType.DMA((PEERS + RELAYED,)), pltpu.SemaphoreType.DMA((RELAYED,)),
            pltpu.SemaphoreType.DMA((2,)), pltpu.SemaphoreType.DMA((2, CHUNKS)),
        ],
        compiler_params=pltpu.CompilerParams(
            collective_id=0, has_side_effects=True, vmem_limit_bytes=56 * 2**20
        ),
    )(
        scale_exp.reshape(3, PEERS),
        qkv[0].transpose(1, 0, 2),
        residual_in[0],
        skip_in[0],
        skip_gain.reshape(1, HD),
    )
    return combined[None]


def solution(mesh):
    return jax.shard_map(
        body,
        mesh=mesh,
        in_specs=(
            P("section", "seq", None, None),
            P("section", "seq", None, None),
            P("section", "seq", None),
            P("section", "seq", None),
            P(),
        ),
        out_specs=P("section", "seq", None),
        check_vma=False,
    )
```

```python
import math

import jax
import jax.numpy as jnp
from jax import lax
from jax.experimental import pallas as pl
from jax.experimental.pallas import tpu as pltpu
from jax.sharding import PartitionSpec as P

MESH = pl.DeviceIdType.MESH
PEERS = 32
HS = 128
ROWS = 128
TOKENS = PEERS * ROWS
HD = PEERS * HS
SECTIONS = 8
RELAYED = 16
LAG = 10
CHUNK_GROUP = 4
PARTS = 8
CHUNKS = 8
GROUP = 2
QB = GROUP * ROWS
KB = 512
LOG2E = math.log2(math.e)
SCORE = LOG2E / math.sqrt(HS)


def pick(i, values):
    out = values[-1]
    for n in range(len(values) - 2, -1, -1):
        out = jnp.where(i == n, values[n], out)
    return out


def offsets(slot):
    dz = jnp.where(slot < RELAYED, 2 - slot % 2, 3 - 3 * (slot % 2))
    return pick((slot // 2) % 4, (2, 1, 3, 0)), dz, 1 - (slot // 8) % 2


def shifted(seq, slot, sign, way):
    dx, dz, dc = offsets(slot)
    x, z, core = seq // 8, (seq // 2) % 4, seq % 2
    return ((x + 4 + way * dx) % 4) * 8 + ((z + 4 + way * sign * dz) % 4) * 2 + (core + dc) % 2


def target(seq, slot, sign):
    return shifted(seq, slot, sign, 1)


def origin(seq, slot, sign):
    return shifted(seq, slot, sign, -1)


def pieces(src, dst, sem):
    for i in range(PARTS):
        rows = pl.ds(i * (ROWS // PARTS), ROWS // PARTS)
        pltpu.make_async_copy(src.at[rows], dst.at[rows], sem).start()


def kernel(
    exps, qkv_hbm, res_hbm, skip_hbm, gain, base, o_in,
    qkv, kv_out, q_out, kv_in, q_in, o_out, o_relay, passed, res_in, skip_in, own_a, own_b, both, scores,
    load_sem, own_sem, kv_send, kv_recv, q_send, q_recv, o_send, o_recv, relay_recv, pass_send, res_sem, skip_sem,
):
    sec = lax.axis_index("section")
    seq = lax.axis_index("seq")
    nxt = (sec + 1) % SECTIONS
    prv = (sec + SECTIONS - 1) % SECTIONS
    mir = SECTIONS - 1 - sec
    sign = 1 - 2 * (sec // 4)
    sums = nxt == mir
    summed = prv == mir

    for c in range(3):
        pieces(qkv_hbm.at[c], qkv.at[c], load_sem)
    res_in[...] = jnp.zeros_like(res_in)
    skip_in[...] = jnp.zeros_like(skip_in)
    barrier = pltpu.get_barrier_semaphore()

    def greet(k, _):
        pl.semaphore_signal(barrier, inc=1, device_id=(sec, target(seq, k, sign)), device_id_type=MESH)
        return 0

    def greet_relay(k, _):
        pl.semaphore_signal(barrier, inc=1, device_id=(mir, origin(seq, k, sign)), device_id_type=MESH)
        return 0

    lax.fori_loop(0, PEERS - 1, greet, 0)
    lax.fori_loop(0, RELAYED, greet_relay, 0)
    for s in (nxt, prv, mir):
        pl.semaphore_signal(barrier, inc=1, device_id=(s, seq), device_id_type=MESH)

    pieces(res_hbm, own_a, own_sem.at[0])
    pieces(skip_hbm, own_b, own_sem.at[1])
    pltpu.make_async_copy(qkv_hbm, qkv, load_sem).wait()

    def scale(k, _):
        head = target(seq, k, sign)
        cols = pl.ds(pl.multiple_of(head * HS, HS), HS)
        for c in range(3):
            power = jnp.left_shift(jnp.int32(1), exps[c, 0, head] + 8).astype(jnp.float32) * (2.0**-8)
            part = (qkv[c, :, cols].astype(jnp.float32) * power).astype(jnp.bfloat16)
            if c == 0:
                q_out[k] = part
            else:
                kv_out[k, c - 1] = part
        return 0

    lax.fori_loop(0, PEERS, scale, 0)
    kv_in[PEERS - 1] = kv_out[PEERS - 1]
    q_in[PEERS - 1] = q_out[PEERS - 1]
    pl.semaphore_wait(barrier, PEERS - 1 + RELAYED + 3)

    def kv_copy(k):
        return pltpu.make_async_remote_copy(
            src_ref=kv_out.at[k], dst_ref=kv_in.at[k], send_sem=kv_send.at[k], recv_sem=kv_recv.at[k],
            device_id=(sec, target(seq, k, sign)), device_id_type=MESH,
        )

    def q_copy(k):
        return pltpu.make_async_remote_copy(
            src_ref=q_out.at[k], dst_ref=q_in.at[k], send_sem=q_send.at[k], recv_sem=q_recv.at[k],
            device_id=(sec, target(seq, k, sign)), device_id_type=MESH,
        )

    def columns(k):
        return pl.ds(pl.multiple_of(target(seq, k, sign) * HS, HS), HS)

    def o_copy(k):
        return pltpu.make_async_remote_copy(
            src_ref=o_out.at[k], dst_ref=o_in.at[:, pl.ds(pl.multiple_of(seq * HS, HS), HS)],
            send_sem=o_send.at[k], recv_sem=o_recv.at[k],
            device_id=(sec, origin(seq, k, sign)), device_id_type=MESH,
        )

    def o_copy_relayed(k):
        return pltpu.make_async_remote_copy(
            src_ref=o_out.at[k], dst_ref=o_relay.at[k], send_sem=o_send.at[k], recv_sem=relay_recv.at[k],
            device_id=(mir, origin(seq, k, sign)), device_id_type=MESH,
        )

    def pass_copy(k):
        cols = pl.ds(pl.multiple_of(target(seq, k, -sign) * HS, HS), HS)
        return pltpu.make_async_remote_copy(
            src_ref=passed.at[k], dst_ref=o_in.at[:, cols], send_sem=pass_send.at[k], recv_sem=o_recv.at[k],
            device_id=(mir, seq), device_id_type=MESH,
        )

    res_copy = pltpu.make_async_remote_copy(
        src_ref=own_a, dst_ref=res_in, send_sem=res_sem.at[0], recv_sem=res_sem.at[1],
        device_id=(nxt, seq), device_id_type=MESH,
    )

    def chunk_copy(i, src, dst):
        z = (seq // 2 + 4 - 3 * sign * (i % 2)) % 4
        cols = pl.ds(pl.multiple_of(((i // 2) * 8 + z * 2) * HS, 2 * HS), 2 * HS)
        return pltpu.make_async_remote_copy(
            src_ref=src.at[:, cols], dst_ref=dst.at[:, cols], send_sem=skip_sem.at[0, i], recv_sem=skip_sem.at[1, i],
            device_id=(mir, seq), device_id_type=MESH,
        )

    def relay(k):
        o_copy_relayed(k).wait_recv()
        cols = pl.ds(pl.multiple_of(target(seq, k, -sign) * HS, HS), HS)
        part = o_relay[k].astype(jnp.float32) + gain[:, cols] * own_b[:, cols].astype(jnp.float32)

        @pl.when(sums)
        def _():
            passed[k] = (part + own_a[:, cols].astype(jnp.float32)).astype(jnp.bfloat16)

        @pl.when(jnp.logical_not(sums))
        def _():
            passed[k] = part.astype(jnp.bfloat16)

        pass_copy(k).start()

    def start_kv(k, _):
        kv_copy((k % 2) * RELAYED + k // 2).start()
        return 0

    def start_q(k, _):
        q_copy(k).start()
        return 0

    lax.fori_loop(0, PEERS - 1, start_kv, 0)
    pltpu.make_async_copy(res_hbm, own_a, own_sem.at[0]).wait()
    pltpu.make_async_copy(skip_hbm, own_b, own_sem.at[1]).wait()

    @pl.when(jnp.logical_not(sums))
    def _():
        res_copy.start()

    lax.fori_loop(0, PEERS - 1, start_q, 0)

    @pl.when(sums)
    def _():
        def add(i, _):
            rows = pl.ds(pl.multiple_of(i * 16, 16), 16)
            total = own_a[rows, :].astype(jnp.float32) + gain[...] * own_b[rows, :].astype(jnp.float32)
            both[rows, :] = total.astype(jnp.bfloat16)
            return 0

        lax.fori_loop(0, ROWS // 16, add, 0)

    def take_kv(k, _):
        kv_copy(k).wait_recv()
        return 0

    lax.fori_loop(0, PEERS - 1, take_kv, 0)

    def attend(g, _):
        first = g * GROUP
        for n in range(GROUP):

            @pl.when(first + n < PEERS - 1)
            def _():
                q_copy(first + n).wait_recv()

        q = q_in[pl.ds(first, GROUP)].reshape(QB, HS)
        most = None
        for j in range(TOKENS // KB):
            keys = kv_in[j * KB // ROWS : (j + 1) * KB // ROWS, 0].reshape(KB, HS)
            s = lax.dot_general(q, keys, (((1,), (1,)), ((), ())), preferred_element_type=jnp.float32)
            scores[:, j * KB : (j + 1) * KB] = s
            for u in range(KB // 128):
                t = s[:, u * 128 : (u + 1) * 128]
                most = t if most is None else jnp.maximum(most, t)
        top = jnp.max(most, axis=1, keepdims=True) * SCORE
        acc = jnp.zeros((QB, HS), jnp.float32)
        total = jnp.zeros((QB, 128), jnp.float32)
        for j in range(TOKENS // KB):
            values = kv_in[j * KB // ROWS : (j + 1) * KB // ROWS, 1].reshape(KB, HS)
            p = jnp.exp2(scores[:, j * KB : (j + 1) * KB] * SCORE - top)
            for u in range(KB // 128):
                total = total + p[:, u * 128 : (u + 1) * 128]
            acc = acc + jnp.dot(p.astype(jnp.bfloat16), values, preferred_element_type=jnp.float32)
        done = (acc / jnp.sum(total, axis=1, keepdims=True)).astype(jnp.bfloat16)
        o_out[pl.ds(first, GROUP)] = done.reshape(GROUP, ROWS, HS)
        for n in range(GROUP):

            @pl.when(first + n < RELAYED)
            def _():
                o_copy_relayed(first + n).start()

            @pl.when(jnp.logical_and(first + n >= RELAYED, first + n < PEERS - 1))
            def _():
                o_copy(first + n).start()

        @pl.when(jnp.logical_and(jnp.logical_and(g >= CHUNK_GROUP, g < CHUNK_GROUP + CHUNKS), sums))
        def _():
            chunk_copy(g - CHUNK_GROUP, both, res_in).start()

        @pl.when(jnp.logical_and(jnp.logical_and(g >= CHUNK_GROUP, g < CHUNK_GROUP + CHUNKS), jnp.logical_not(sums)))
        def _():
            chunk_copy(g - CHUNK_GROUP, own_b, skip_in).start()

        @pl.when(g >= LAG)
        def _():
            for n in range(GROUP):
                relay((g - LAG) * GROUP + n)

        return 0

    lax.fori_loop(0, PEERS // GROUP, attend, 0)

    def relay_late(k, _):
        relay(k)
        return 0

    lax.fori_loop(PEERS - LAG * GROUP, RELAYED, relay_late, 0)
    o_in[:, columns(PEERS - 1)] = o_out[PEERS - 1]

    @pl.when(jnp.logical_not(summed))
    def _():
        res_copy.wait_recv()

    def take_chunk(i, _):
        chunk_copy(i, own_b, skip_in).wait_recv()
        return 0

    lax.fori_loop(0, CHUNKS, take_chunk, 0)

    def gather(i, _):
        rows = pl.ds(pl.multiple_of(i * 16, 16), 16)
        base[rows, :] = res_in[rows, :].astype(jnp.float32) + gain[...] * skip_in[rows, :].astype(jnp.float32)
        return 0

    lax.fori_loop(0, ROWS // 16, gather, 0)

    def take_o(k, _):
        o_copy(k).wait_recv()
        return 0

    lax.fori_loop(0, PEERS - 1, take_o, 0)

    def sent(k, _):
        kv_copy(k).wait_send()
        q_copy(k).wait_send()
        o_copy(k).wait_send()
        return 0

    def sent_more(k, _):
        pass_copy(k).wait_send()
        return 0

    def sent_chunk(i, _):
        chunk_copy(i, own_b, skip_in).wait_send()
        return 0

    lax.fori_loop(0, PEERS - 1, sent, 0)
    lax.fori_loop(0, RELAYED, sent_more, 0)
    lax.fori_loop(0, CHUNKS, sent_chunk, 0)

    @pl.when(jnp.logical_not(sums))
    def _():
        res_copy.wait_send()


def body(qkv, scale_exp, residual_in, skip_in, skip_gain):
    bf16 = jnp.bfloat16
    block = pltpu.VMEM((PEERS, ROWS, HS), bf16)
    pair = pltpu.VMEM((PEERS, 2, ROWS, HS), bf16)
    rows = pltpu.VMEM((ROWS, HD), bf16)
    sems = pltpu.SemaphoreType.DMA((PEERS,))
    anywhere = pl.BlockSpec(memory_space=pl.ANY)
    vmem = pl.BlockSpec(memory_space=pltpu.VMEM)
    base, done = pl.pallas_call(
        kernel,
        out_shape=(pltpu.VMEM((ROWS, HD), jnp.float32), rows),
        in_specs=[pl.BlockSpec(memory_space=pltpu.SMEM), anywhere, anywhere, anywhere, vmem],
        out_specs=(vmem, vmem),
        scratch_shapes=[
            pltpu.VMEM((3, ROWS, HD), bf16), pair, block, pair, block, block,
            pltpu.VMEM((RELAYED, ROWS, HS), bf16), pltpu.VMEM((RELAYED, ROWS, HS), bf16), rows, rows, rows, rows, rows,
            pltpu.VMEM((QB, TOKENS), jnp.float32),
            pltpu.SemaphoreType.DMA, pltpu.SemaphoreType.DMA((2,)), sems, sems, sems, sems, sems,
            sems, pltpu.SemaphoreType.DMA((RELAYED,)), pltpu.SemaphoreType.DMA((RELAYED,)),
            pltpu.SemaphoreType.DMA((2,)), pltpu.SemaphoreType.DMA((2, CHUNKS)),
        ],
        compiler_params=pltpu.CompilerParams(
            collective_id=0, has_side_effects=True, vmem_limit_bytes=56 * 2**20
        ),
    )(
        scale_exp[0].transpose(1, 0, 2),
        qkv[0].transpose(1, 0, 2),
        residual_in[0],
        skip_in[0],
        skip_gain.reshape(1, HD),
    )
    return (base + done.astype(jnp.float32)).astype(bf16)[None]


def solution(mesh):
    return jax.shard_map(
        body,
        mesh=mesh,
        in_specs=(
            P("section", "seq", None, None),
            P("section", "seq", None, None),
            P("section", "seq", None),
            P("section", "seq", None),
            P(),
        ),
        out_specs=P("section", "seq", None),
        check_vma=False,
    )
```

```python
import math

import jax
import jax.numpy as jnp
from jax import lax
from jax.experimental import pallas as pl
from jax.experimental.pallas import tpu as pltpu
from jax.sharding import PartitionSpec as P

MESH = pl.DeviceIdType.MESH
PEERS = 32
HS = 128
ROWS = 128
TOKENS = PEERS * ROWS
HD = PEERS * HS
SECTIONS = 8
RELAYED = 16
LAG = 12
CHUNK_GROUP = 4
EARLY = 8
CHUNKS = 8
GROUP = 2
QB = GROUP * ROWS
KB = 512
LOG2E = math.log2(math.e)
SCORE = LOG2E / math.sqrt(HS)


def pick(i, values):
    out = values[-1]
    for n in range(len(values) - 2, -1, -1):
        out = jnp.where(i == n, values[n], out)
    return out


def offsets(slot):
    dz = jnp.where(slot < RELAYED, 2 - slot % 2, 3 - 3 * (slot % 2))
    return pick((slot // 2) % 4, (2, 1, 3, 0)), dz, 1 - (slot // 8) % 2


def shifted(seq, slot, sign, way):
    dx, dz, dc = offsets(slot)
    x, z, core = seq // 8, (seq // 2) % 4, seq % 2
    return ((x + 4 + way * dx) % 4) * 8 + ((z + 4 + way * sign * dz) % 4) * 2 + (core + dc) % 2


def target(seq, slot, sign):
    return shifted(seq, slot, sign, 1)


def origin(seq, slot, sign):
    return shifted(seq, slot, sign, -1)


def kernel(
    exps, qkv_hbm, res_hbm, skip_hbm, gain, base, o_in,
    qkv, kv_out, q_out, kv_in, q_in, o_out, o_relay, passed, res_in, skip_in, own_a, own_b, both, scores,
    load_sem, own_sem, kv_send, kv_recv, q_send, q_recv, o_send, o_recv, relay_recv, pass_send, res_sem, skip_sem,
):
    sec = lax.axis_index("section")
    seq = lax.axis_index("seq")
    nxt = (sec + 1) % SECTIONS
    prv = (sec + SECTIONS - 1) % SECTIONS
    mir = SECTIONS - 1 - sec
    sign = 1 - 2 * (sec // 4)
    sums = nxt == mir
    summed = prv == mir

    load = pltpu.make_async_copy(qkv_hbm, qkv, load_sem)
    own_res = pltpu.make_async_copy(res_hbm, own_a, own_sem.at[0])
    own_skip = pltpu.make_async_copy(skip_hbm, own_b, own_sem.at[1])
    load.start()
    barrier = pltpu.get_barrier_semaphore()

    for k in range(1, PEERS):
        pl.semaphore_signal(barrier, inc=1, device_id=(sec, (seq + k) % PEERS), device_id_type=MESH)
    for a in (1, 2):
        z = (seq // 2 + 4 - sign * a) % 4
        for k in range(8):
            peer = (k // 2) * 8 + z * 2 + k % 2
            pl.semaphore_signal(barrier, inc=1, device_id=(mir, peer), device_id_type=MESH)
    for s in (nxt, prv, mir):
        pl.semaphore_signal(barrier, inc=1, device_id=(s, seq), device_id_type=MESH)

    own_res.start()
    own_skip.start()
    load.wait()

    def scaled(k, c):
        head = target(seq, k, sign)
        cols = pl.ds(pl.multiple_of(head * HS, HS), HS)
        power = jnp.left_shift(jnp.int32(1), exps[c, 0, head] + 8).astype(jnp.float32) * (2.0**-8)
        return (qkv[c, :, cols].astype(jnp.float32) * power).astype(jnp.bfloat16)

    def kv_slot(i):
        return (i % 2) * RELAYED + i // 2

    def scale_kv(i, _):
        k = kv_slot(i)
        kv_out[k, 0] = scaled(k, 1)
        kv_out[k, 1] = scaled(k, 2)
        return 0

    lax.fori_loop(0, EARLY, scale_kv, 0)

    pl.semaphore_wait(barrier, PEERS - 1 + RELAYED + 3)

    def kv_copy(k):
        return pltpu.make_async_remote_copy(
            src_ref=kv_out.at[k], dst_ref=kv_in.at[k], send_sem=kv_send.at[k], recv_sem=kv_recv.at[k],
            device_id=(sec, target(seq, k, sign)), device_id_type=MESH,
        )

    def q_copy(k):
        return pltpu.make_async_remote_copy(
            src_ref=q_out.at[k], dst_ref=q_in.at[k], send_sem=q_send.at[k], recv_sem=q_recv.at[k],
            device_id=(sec, target(seq, k, sign)), device_id_type=MESH,
        )

    def columns(k):
        return pl.ds(pl.multiple_of(target(seq, k, sign) * HS, HS), HS)

    def o_copy(k):
        return pltpu.make_async_remote_copy(
            src_ref=o_out.at[k], dst_ref=o_in.at[:, pl.ds(pl.multiple_of(seq * HS, HS), HS)],
            send_sem=o_send.at[k], recv_sem=o_recv.at[k],
            device_id=(sec, origin(seq, k, sign)), device_id_type=MESH,
        )

    def o_copy_relayed(k):
        return pltpu.make_async_remote_copy(
            src_ref=o_out.at[k], dst_ref=o_relay.at[k], send_sem=o_send.at[k], recv_sem=relay_recv.at[k],
            device_id=(mir, origin(seq, k, sign)), device_id_type=MESH,
        )

    def pass_copy(k):
        cols = pl.ds(pl.multiple_of(target(seq, k, -sign) * HS, HS), HS)
        return pltpu.make_async_remote_copy(
            src_ref=passed.at[k], dst_ref=o_in.at[:, cols], send_sem=pass_send.at[k], recv_sem=o_recv.at[k],
            device_id=(mir, seq), device_id_type=MESH,
        )

    res_copy = pltpu.make_async_remote_copy(
        src_ref=own_a, dst_ref=res_in, send_sem=res_sem.at[0], recv_sem=res_sem.at[1],
        device_id=(nxt, seq), device_id_type=MESH,
    )

    def chunk_copy(i, src, dst):
        z = (seq // 2 + 4 - 3 * sign * (i % 2)) % 4
        cols = pl.ds(pl.multiple_of(((i // 2) * 8 + z * 2) * HS, 2 * HS), 2 * HS)
        return pltpu.make_async_remote_copy(
            src_ref=src.at[:, cols], dst_ref=dst.at[:, cols], send_sem=skip_sem.at[0, i], recv_sem=skip_sem.at[1, i],
            device_id=(mir, seq), device_id_type=MESH,
        )

    def relay(k):
        o_copy_relayed(k).wait_recv()
        cols = pl.ds(pl.multiple_of(target(seq, k, -sign) * HS, HS), HS)
        part = o_relay[k].astype(jnp.float32) + gain[:, cols] * own_b[:, cols].astype(jnp.float32)

        @pl.when(sums)
        def _():
            passed[k] = (part + own_a[:, cols].astype(jnp.float32)).astype(jnp.bfloat16)

        @pl.when(jnp.logical_not(sums))
        def _():
            passed[k] = part.astype(jnp.bfloat16)

        pass_copy(k).start()

    def start_kv(i, _):
        kv_copy(kv_slot(i)).start()
        return 0

    def scale_start_kv(i, _):
        scale_kv(i, 0)
        return start_kv(i, 0)

    def scale_start_q(k, _):
        q_out[k] = scaled(k, 0)
        q_copy(k).start()
        return 0

    lax.fori_loop(0, EARLY, start_kv, 0)
    lax.fori_loop(EARLY, PEERS - 1, scale_start_kv, 0)
    own_res.wait()
    own_skip.wait()

    @pl.when(jnp.logical_not(sums))
    def _():
        res_copy.start()

    lax.fori_loop(0, PEERS - 1, scale_start_q, 0)
    kv_in[PEERS - 1, 0] = scaled(PEERS - 1, 1)
    kv_in[PEERS - 1, 1] = scaled(PEERS - 1, 2)
    q_in[PEERS - 1] = scaled(PEERS - 1, 0)

    @pl.when(sums)
    def _():
        def add(i, _):
            rows = pl.ds(pl.multiple_of(i * 16, 16), 16)
            total = own_a[rows, :].astype(jnp.float32) + gain[...] * own_b[rows, :].astype(jnp.float32)
            both[rows, :] = total.astype(jnp.bfloat16)
            return 0

        lax.fori_loop(0, ROWS // 16, add, 0)

    def take_kv(k, _):
        kv_copy(k).wait_recv()
        return 0

    lax.fori_loop(0, PEERS - 1, take_kv, 0)

    def attend(g, _):
        first = g * GROUP
        for n in range(GROUP):

            @pl.when(first + n < PEERS - 1)
            def _():
                q_copy(first + n).wait_recv()

        q = q_in[pl.ds(first, GROUP)].reshape(QB, HS)
        most = None
        for j in range(TOKENS // KB):
            keys = kv_in[j * KB // ROWS : (j + 1) * KB // ROWS, 0].reshape(KB, HS)
            s = lax.dot_general(q, keys, (((1,), (1,)), ((), ())), preferred_element_type=jnp.float32)
            scores[:, j * KB : (j + 1) * KB] = s
            for u in range(KB // 128):
                t = s[:, u * 128 : (u + 1) * 128]
                most = t if most is None else jnp.maximum(most, t)
        top = jnp.max(most, axis=1, keepdims=True) * SCORE
        acc = jnp.zeros((QB, HS), jnp.float32)
        total = jnp.zeros((QB, 128), jnp.float32)
        for j in range(TOKENS // KB):
            values = kv_in[j * KB // ROWS : (j + 1) * KB // ROWS, 1].reshape(KB, HS)
            p = jnp.exp2(scores[:, j * KB : (j + 1) * KB] * SCORE - top)
            for u in range(KB // 128):
                total = total + p[:, u * 128 : (u + 1) * 128]
            acc = acc + jnp.dot(p.astype(jnp.bfloat16), values, preferred_element_type=jnp.float32)
        done = (acc / jnp.sum(total, axis=1, keepdims=True)).astype(jnp.bfloat16)
        o_out[pl.ds(first, GROUP)] = done.reshape(GROUP, ROWS, HS)
        for n in range(GROUP):

            @pl.when(first + n < RELAYED)
            def _():
                o_copy_relayed(first + n).start()

            @pl.when(jnp.logical_and(first + n >= RELAYED, first + n < PEERS - 1))
            def _():
                o_copy(first + n).start()

        @pl.when(jnp.logical_and(jnp.logical_and(g >= CHUNK_GROUP, g < CHUNK_GROUP + CHUNKS), sums))
        def _():
            chunk_copy(g - CHUNK_GROUP, both, res_in).start()

        @pl.when(jnp.logical_and(jnp.logical_and(g >= CHUNK_GROUP, g < CHUNK_GROUP + CHUNKS), jnp.logical_not(sums)))
        def _():
            chunk_copy(g - CHUNK_GROUP, own_b, skip_in).start()

        @pl.when(g >= LAG)
        def _():
            for n in range(GROUP):
                relay((g - LAG) * GROUP + n)

        return 0

    lax.fori_loop(0, PEERS // GROUP, attend, 0)

    def relay_late(k, _):
        relay(k)
        return 0

    lax.fori_loop(PEERS - LAG * GROUP, RELAYED, relay_late, 0)
    o_in[:, columns(PEERS - 1)] = o_out[PEERS - 1]

    @pl.when(jnp.logical_not(summed))
    def _():
        res_copy.wait_recv()

    def sent_early(k, _):
        kv_copy(k).wait_send()
        q_copy(k).wait_send()
        return 0

    lax.fori_loop(0, PEERS - 1, sent_early, 0)

    @pl.when(jnp.logical_not(sums))
    def _():
        res_copy.wait_send()

    def take_chunk(i, _):
        chunk_copy(i, own_b, skip_in).wait_recv()
        return 0

    lax.fori_loop(0, CHUNKS, take_chunk, 0)

    def gather(i, _):
        step = (sign * (i % 4 - (seq // 2) % 4) + 4) % 4
        relayed = jnp.logical_or(step == 1, step == 2)
        cols = pl.ds(pl.multiple_of(i * 2 * HS, 2 * HS), 2 * HS)

        @pl.when(jnp.logical_and(relayed, summed))
        def _():
            base[:, cols] = jnp.zeros((ROWS, 2 * HS), jnp.float32)

        @pl.when(jnp.logical_xor(relayed, summed))
        def _():
            base[:, cols] = res_in[:, cols].astype(jnp.float32)

        @pl.when(jnp.logical_not(jnp.logical_or(relayed, summed)))
        def _():
            base[:, cols] = res_in[:, cols].astype(jnp.float32) + gain[:, cols] * skip_in[:, cols].astype(jnp.float32)

        return 0

    lax.fori_loop(0, PEERS // 2, gather, 0)

    def sent(k, _):
        o_copy(k).wait_send()
        return 0

    def sent_more(k, _):
        pass_copy(k).wait_send()
        return 0

    def sent_chunk(i, _):
        chunk_copy(i, own_b, skip_in).wait_send()
        return 0

    lax.fori_loop(0, CHUNKS, sent_chunk, 0)
    lax.fori_loop(0, PEERS - 1, sent, 0)
    lax.fori_loop(0, RELAYED, sent_more, 0)

    def take_o(k, _):
        o_copy(k).wait_recv()
        return 0

    lax.fori_loop(RELAYED, PEERS - 1, take_o, 0)
    lax.fori_loop(0, RELAYED, take_o, 0)


def body(qkv, scale_exp, residual_in, skip_in, skip_gain):
    bf16 = jnp.bfloat16
    block = pltpu.VMEM((PEERS, ROWS, HS), bf16)
    pair = pltpu.VMEM((PEERS, 2, ROWS, HS), bf16)
    rows = pltpu.VMEM((ROWS, HD), bf16)
    sems = pltpu.SemaphoreType.DMA((PEERS,))
    anywhere = pl.BlockSpec(memory_space=pl.ANY)
    vmem = pl.BlockSpec(memory_space=pltpu.VMEM)
    base, done = pl.pallas_call(
        kernel,
        out_shape=(pltpu.VMEM((ROWS, HD), jnp.float32), rows),
        in_specs=[pl.BlockSpec(memory_space=pltpu.SMEM), anywhere, anywhere, anywhere, vmem],
        out_specs=(vmem, vmem),
        scratch_shapes=[
            pltpu.VMEM((3, ROWS, HD), bf16), pair, block, pair, block, block,
            pltpu.VMEM((RELAYED, ROWS, HS), bf16), pltpu.VMEM((RELAYED, ROWS, HS), bf16), rows, rows, rows, rows, rows,
            pltpu.VMEM((QB, TOKENS), jnp.float32),
            pltpu.SemaphoreType.DMA, pltpu.SemaphoreType.DMA((2,)), sems, sems, sems, sems, sems,
            sems, pltpu.SemaphoreType.DMA((RELAYED,)), pltpu.SemaphoreType.DMA((RELAYED,)),
            pltpu.SemaphoreType.DMA((2,)), pltpu.SemaphoreType.DMA((2, CHUNKS)),
        ],
        compiler_params=pltpu.CompilerParams(
            collective_id=0, has_side_effects=True, vmem_limit_bytes=56 * 2**20
        ),
    )(
        scale_exp[0].transpose(1, 0, 2),
        qkv[0].transpose(1, 0, 2),
        residual_in[0],
        skip_in[0],
        skip_gain.reshape(1, HD),
    )
    return (base + done.astype(jnp.float32)).astype(bf16)[None]


def solution(mesh):
    return jax.shard_map(
        body,
        mesh=mesh,
        in_specs=(
            P("section", "seq", None, None),
            P("section", "seq", None, None),
            P("section", "seq", None),
            P("section", "seq", None),
            P(),
        ),
        out_specs=P("section", "seq", None),
        check_vma=False,
    )
```

```python
import math

import jax
import jax.numpy as jnp
from jax import lax
from jax.experimental import pallas as pl
from jax.experimental.pallas import tpu as pltpu
from jax.sharding import PartitionSpec as P

MESH = pl.DeviceIdType.MESH
PEERS = 32
HS = 128
ROWS = 128
TOKENS = PEERS * ROWS
HD = PEERS * HS
SECTIONS = 8
RELAYED = 16
LAG = 12
CHUNK_GROUP = 4
EARLY = 3
CHUNKS = 8
GROUP = 2
QB = GROUP * ROWS
KB = 512
LOG2E = math.log2(math.e)
SCORE = LOG2E / math.sqrt(HS)


def pick(i, values):
    out = values[-1]
    for n in range(len(values) - 2, -1, -1):
        out = jnp.where(i == n, values[n], out)
    return out


def offsets(slot):
    dz = jnp.where(slot < RELAYED, 2 - slot % 2, 3 - 3 * (slot % 2))
    return pick((slot // 2) % 4, (2, 1, 3, 0)), dz, 1 - (slot // 8) % 2


def shifted(seq, slot, sign, way):
    dx, dz, dc = offsets(slot)
    x, z, core = seq // 8, (seq // 2) % 4, seq % 2
    return ((x + 4 + way * dx) % 4) * 8 + ((z + 4 + way * sign * dz) % 4) * 2 + (core + dc) % 2


def target(seq, slot, sign):
    return shifted(seq, slot, sign, 1)


def origin(seq, slot, sign):
    return shifted(seq, slot, sign, -1)


def kernel(
    exps, qkv_hbm, res_hbm, skip_hbm, gain, base, o_in,
    qkv, kv_out, q_out, kv_in, q_in, o_out, o_relay, passed, res_in, skip_in, own_a, own_b, both, scores,
    load_sem, own_sem, kv_send, kv_recv, q_send, q_recv, o_send, o_recv, relay_recv, pass_send, res_sem, skip_sem,
):
    sec = lax.axis_index("section")
    seq = lax.axis_index("seq")
    nxt = (sec + 1) % SECTIONS
    prv = (sec + SECTIONS - 1) % SECTIONS
    mir = SECTIONS - 1 - sec
    sign = 1 - 2 * (sec // 4)
    sums = nxt == mir
    summed = prv == mir

    load_kv = pltpu.make_async_copy(qkv_hbm.at[pl.ds(1, 2)], qkv.at[pl.ds(1, 2)], load_sem.at[0])
    load_q = pltpu.make_async_copy(qkv_hbm.at[0], qkv.at[0], load_sem.at[1])
    own_res = pltpu.make_async_copy(res_hbm, own_a, own_sem.at[0])
    own_skip = pltpu.make_async_copy(skip_hbm, own_b, own_sem.at[1])
    load_kv.start()
    barrier = pltpu.get_barrier_semaphore()

    for k in range(1, PEERS):
        pl.semaphore_signal(barrier, inc=1, device_id=(sec, (seq + k) % PEERS), device_id_type=MESH)
    for a in (1, 2):
        z = (seq // 2 + 4 - sign * a) % 4
        for k in range(8):
            peer = (k // 2) * 8 + z * 2 + k % 2
            pl.semaphore_signal(barrier, inc=1, device_id=(mir, peer), device_id_type=MESH)
    for s in (nxt, prv, mir):
        pl.semaphore_signal(barrier, inc=1, device_id=(s, seq), device_id_type=MESH)

    load_q.start()
    own_res.start()
    own_skip.start()
    load_kv.wait()

    def scaled(k, c):
        head = target(seq, k, sign)
        cols = pl.ds(pl.multiple_of(head * HS, HS), HS)
        power = jnp.left_shift(jnp.int32(1), exps[c, 0, head] + 8).astype(jnp.float32) * (2.0**-8)
        return (qkv[c, :, cols].astype(jnp.float32) * power).astype(jnp.bfloat16)

    def kv_slot(i):
        return (i % 2) * RELAYED + i // 2

    def scale_kv(i, _):
        k = kv_slot(i)
        kv_out[k, 0] = scaled(k, 1)
        kv_out[k, 1] = scaled(k, 2)
        return 0

    lax.fori_loop(0, EARLY, scale_kv, 0)

    pl.semaphore_wait(barrier, PEERS - 1 + RELAYED + 3)

    def kv_copy(k):
        return pltpu.make_async_remote_copy(
            src_ref=kv_out.at[k], dst_ref=kv_in.at[k], send_sem=kv_send.at[k], recv_sem=kv_recv.at[k],
            device_id=(sec, target(seq, k, sign)), device_id_type=MESH,
        )

    def q_copy(k):
        return pltpu.make_async_remote_copy(
            src_ref=q_out.at[k], dst_ref=q_in.at[k], send_sem=q_send.at[k], recv_sem=q_recv.at[k],
            device_id=(sec, target(seq, k, sign)), device_id_type=MESH,
        )

    def columns(k):
        return pl.ds(pl.multiple_of(target(seq, k, sign) * HS, HS), HS)

    def o_copy(k):
        return pltpu.make_async_remote_copy(
            src_ref=o_out.at[k], dst_ref=o_in.at[:, pl.ds(pl.multiple_of(seq * HS, HS), HS)],
            send_sem=o_send.at[k], recv_sem=o_recv.at[k],
            device_id=(sec, origin(seq, k, sign)), device_id_type=MESH,
        )

    def o_copy_relayed(k):
        return pltpu.make_async_remote_copy(
            src_ref=o_out.at[k], dst_ref=o_relay.at[k], send_sem=o_send.at[k], recv_sem=relay_recv.at[k],
            device_id=(mir, origin(seq, k, sign)), device_id_type=MESH,
        )

    def pass_copy(k):
        cols = pl.ds(pl.multiple_of(target(seq, k, -sign) * HS, HS), HS)
        return pltpu.make_async_remote_copy(
            src_ref=passed.at[k], dst_ref=o_in.at[:, cols], send_sem=pass_send.at[k], recv_sem=o_recv.at[k],
            device_id=(mir, seq), device_id_type=MESH,
        )

    res_copy = pltpu.make_async_remote_copy(
        src_ref=own_a, dst_ref=res_in, send_sem=res_sem.at[0], recv_sem=res_sem.at[1],
        device_id=(nxt, seq), device_id_type=MESH,
    )

    def chunk_copy(i, src, dst):
        z = (seq // 2 + 4 - 3 * sign * (i % 2)) % 4
        cols = pl.ds(pl.multiple_of(((i // 2) * 8 + z * 2) * HS, 2 * HS), 2 * HS)
        return pltpu.make_async_remote_copy(
            src_ref=src.at[:, cols], dst_ref=dst.at[:, cols], send_sem=skip_sem.at[0, i], recv_sem=skip_sem.at[1, i],
            device_id=(mir, seq), device_id_type=MESH,
        )

    def relay(k):
        o_copy_relayed(k).wait_recv()
        cols = pl.ds(pl.multiple_of(target(seq, k, -sign) * HS, HS), HS)
        part = o_relay[k].astype(jnp.float32) + gain[:, cols] * own_b[:, cols].astype(jnp.float32)

        @pl.when(sums)
        def _():
            passed[k] = (part + own_a[:, cols].astype(jnp.float32)).astype(jnp.bfloat16)

        @pl.when(jnp.logical_not(sums))
        def _():
            passed[k] = part.astype(jnp.bfloat16)

        pass_copy(k).start()

    def start_kv(i, _):
        kv_copy(kv_slot(i)).start()
        return 0

    def scale_start_kv(i, _):
        scale_kv(i, 0)
        return start_kv(i, 0)

    def q_slot(i):
        mixed = jnp.where(i % 4 < 3, i - i // 4, RELAYED + i // 4)
        return jnp.where(i < 20, mixed, jnp.where(i == 20, RELAYED - 1, i))

    def scale_start_q(i, _):
        k = q_slot(i)
        q_out[k] = scaled(k, 0)
        q_copy(k).start()
        return 0

    lax.fori_loop(0, EARLY, start_kv, 0)
    lax.fori_loop(EARLY, PEERS - 1, scale_start_kv, 0)
    load_q.wait()
    own_res.wait()
    own_skip.wait()

    @pl.when(jnp.logical_not(sums))
    def _():
        res_copy.start()

    lax.fori_loop(0, PEERS - 1, scale_start_q, 0)
    kv_in[PEERS - 1, 0] = scaled(PEERS - 1, 1)
    kv_in[PEERS - 1, 1] = scaled(PEERS - 1, 2)
    q_in[PEERS - 1] = scaled(PEERS - 1, 0)

    @pl.when(sums)
    def _():
        def add(i, _):
            rows = pl.ds(pl.multiple_of(i * 16, 16), 16)
            total = own_a[rows, :].astype(jnp.float32) + gain[...] * own_b[rows, :].astype(jnp.float32)
            both[rows, :] = total.astype(jnp.bfloat16)
            return 0

        lax.fori_loop(0, ROWS // 16, add, 0)

    def take_kv(k, _):
        kv_copy(k).wait_recv()
        return 0

    lax.fori_loop(0, PEERS - 1, take_kv, 0)

    def attend(g, _):
        first = g * GROUP
        for n in range(GROUP):

            @pl.when(first + n < PEERS - 1)
            def _():
                q_copy(first + n).wait_recv()

        q = q_in[pl.ds(first, GROUP)].reshape(QB, HS)
        most = None
        for j in range(TOKENS // KB):
            keys = kv_in[j * KB // ROWS : (j + 1) * KB // ROWS, 0].reshape(KB, HS)
            s = lax.dot_general(q, keys, (((1,), (1,)), ((), ())), preferred_element_type=jnp.float32)
            scores[:, j * KB : (j + 1) * KB] = s
            for u in range(KB // 128):
                t = s[:, u * 128 : (u + 1) * 128]
                most = t if most is None else jnp.maximum(most, t)
        top = jnp.max(most, axis=1, keepdims=True) * SCORE
        acc = jnp.zeros((QB, HS), jnp.float32)
        total = jnp.zeros((QB, 128), jnp.float32)
        for j in range(TOKENS // KB):
            values = kv_in[j * KB // ROWS : (j + 1) * KB // ROWS, 1].reshape(KB, HS)
            p = jnp.exp2(scores[:, j * KB : (j + 1) * KB] * SCORE - top)
            for u in range(KB // 128):
                total = total + p[:, u * 128 : (u + 1) * 128]
            acc = acc + jnp.dot(p.astype(jnp.bfloat16), values, preferred_element_type=jnp.float32)
        done = (acc / jnp.sum(total, axis=1, keepdims=True)).astype(jnp.bfloat16)
        o_out[pl.ds(first, GROUP)] = done.reshape(GROUP, ROWS, HS)
        for n in range(GROUP):

            @pl.when(first + n < RELAYED)
            def _():
                o_copy_relayed(first + n).start()

            @pl.when(jnp.logical_and(first + n >= RELAYED, first + n < PEERS - 1))
            def _():
                o_copy(first + n).start()

        @pl.when(jnp.logical_and(jnp.logical_and(g >= CHUNK_GROUP, g < CHUNK_GROUP + CHUNKS), sums))
        def _():
            chunk_copy(g - CHUNK_GROUP, both, res_in).start()

        @pl.when(jnp.logical_and(jnp.logical_and(g >= CHUNK_GROUP, g < CHUNK_GROUP + CHUNKS), jnp.logical_not(sums)))
        def _():
            chunk_copy(g - CHUNK_GROUP, own_b, skip_in).start()

        @pl.when(g >= LAG)
        def _():
            for n in range(GROUP):
                relay((g - LAG) * GROUP + n)

        return 0

    lax.fori_loop(0, PEERS // GROUP, attend, 0)

    def relay_late(k, _):
        relay(k)
        return 0

    lax.fori_loop(PEERS - LAG * GROUP, RELAYED, relay_late, 0)
    o_in[:, columns(PEERS - 1)] = o_out[PEERS - 1]

    @pl.when(jnp.logical_not(summed))
    def _():
        res_copy.wait_recv()

    def sent_early(k, _):
        kv_copy(k).wait_send()
        q_copy(k).wait_send()
        return 0

    lax.fori_loop(0, PEERS - 1, sent_early, 0)

    @pl.when(jnp.logical_not(sums))
    def _():
        res_copy.wait_send()

    def take_chunk(i, _):
        chunk_copy(i, own_b, skip_in).wait_recv()
        return 0

    lax.fori_loop(0, CHUNKS, take_chunk, 0)

    def gather(i, _):
        step = (sign * (i % 4 - (seq // 2) % 4) + 4) % 4
        relayed = jnp.logical_or(step == 1, step == 2)
        cols = pl.ds(pl.multiple_of(i * 2 * HS, 2 * HS), 2 * HS)

        @pl.when(jnp.logical_and(relayed, summed))
        def _():
            base[:, cols] = jnp.zeros((ROWS, 2 * HS), jnp.float32)

        @pl.when(jnp.logical_xor(relayed, summed))
        def _():
            base[:, cols] = res_in[:, cols].astype(jnp.float32)

        @pl.when(jnp.logical_not(jnp.logical_or(relayed, summed)))
        def _():
            base[:, cols] = res_in[:, cols].astype(jnp.float32) + gain[:, cols] * skip_in[:, cols].astype(jnp.float32)

        return 0

    lax.fori_loop(0, PEERS // 2, gather, 0)

    def sent(k, _):
        o_copy(k).wait_send()
        return 0

    def sent_more(k, _):
        pass_copy(k).wait_send()
        return 0

    def sent_chunk(i, _):
        chunk_copy(i, own_b, skip_in).wait_send()
        return 0

    lax.fori_loop(0, CHUNKS, sent_chunk, 0)
    lax.fori_loop(0, PEERS - 1, sent, 0)
    lax.fori_loop(0, RELAYED, sent_more, 0)

    def take_o(k, _):
        o_copy(k).wait_recv()
        return 0

    lax.fori_loop(RELAYED, PEERS - 1, take_o, 0)
    lax.fori_loop(0, RELAYED, take_o, 0)


def body(qkv, scale_exp, residual_in, skip_in, skip_gain):
    bf16 = jnp.bfloat16
    block = pltpu.VMEM((PEERS, ROWS, HS), bf16)
    pair = pltpu.VMEM((PEERS, 2, ROWS, HS), bf16)
    rows = pltpu.VMEM((ROWS, HD), bf16)
    sems = pltpu.SemaphoreType.DMA((PEERS,))
    anywhere = pl.BlockSpec(memory_space=pl.ANY)
    vmem = pl.BlockSpec(memory_space=pltpu.VMEM)
    base, done = pl.pallas_call(
        kernel,
        out_shape=(pltpu.VMEM((ROWS, HD), jnp.float32), rows),
        in_specs=[pl.BlockSpec(memory_space=pltpu.SMEM), anywhere, anywhere, anywhere, vmem],
        out_specs=(vmem, vmem),
        scratch_shapes=[
            pltpu.VMEM((3, ROWS, HD), bf16), pair, block, pair, block, block,
            pltpu.VMEM((RELAYED, ROWS, HS), bf16), pltpu.VMEM((RELAYED, ROWS, HS), bf16), rows, rows, rows, rows, rows,
            pltpu.VMEM((QB, TOKENS), jnp.float32),
            pltpu.SemaphoreType.DMA((2,)), pltpu.SemaphoreType.DMA((2,)), sems, sems, sems, sems, sems,
            sems, pltpu.SemaphoreType.DMA((RELAYED,)), pltpu.SemaphoreType.DMA((RELAYED,)),
            pltpu.SemaphoreType.DMA((2,)), pltpu.SemaphoreType.DMA((2, CHUNKS)),
        ],
        compiler_params=pltpu.CompilerParams(
            collective_id=0, has_side_effects=True, vmem_limit_bytes=56 * 2**20
        ),
    )(
        scale_exp[0].transpose(1, 0, 2),
        qkv[0].transpose(1, 0, 2),
        residual_in[0],
        skip_in[0],
        skip_gain.reshape(1, HD),
    )
    return (base + done.astype(jnp.float32)).astype(bf16)[None]


def solution(mesh):
    return jax.shard_map(
        body,
        mesh=mesh,
        in_specs=(
            P("section", "seq", None, None),
            P("section", "seq", None, None),
            P("section", "seq", None),
            P("section", "seq", None),
            P(),
        ),
        out_specs=P("section", "seq", None),
        check_vma=False,
    )
```
